1024 devices in a mesh: row: 32 (over x, z_hi, core), col: 32 (over y, z_lo).
Axes of the slice: x: 4, y: 4, z: 32 (z_hi: 4, z_lo: 8; z = z_hi * 8 + z_lo), core: 2. Of those that a mesh axis runs over, the one named last changes fastest.
Arguments:
- saved_input: float32 [1280, 16384], P('row', 'col'), may hold values from -6 to 6
- out_grad: float32 [1280, 16384], P('col', 'row'), may hold values from -1.2 to 1.2
- weight: bfloat16 [16384, 16384], P('row', 'col'), may hold values from -0.046875 to 0.046875
- history_in: float32 [32, 32, 16], P('row', 'col'), may hold values from 2 to 8
- history_grad: float32 [32, 32, 16], P('row', 'col'), may hold values from 0.4 to 1.6
- slot_in: int32 [32, 32], P('row', 'col'), may hold values from 0 to 15
- slot_grad: int32 [32, 32], P('row', 'col'), may hold values from 0 to 15
- step_count: int32 [1], replicated, may hold values from 1 to 16
Outputs:
- weight_grad: float32 [16384, 16384], P('row', 'col')
- input_grad: bfloat16 [1280, 16384], P('row', 'col')
- new_history_in: float32 [32, 32, 16], P('row', 'col')
- new_history_grad: float32 [32, 32, 16], P('row', 'col')
The draws below stay inside these ranges and needn't reach their ends.
All inputs are finite; a program needn't handle non-finite values.
Results may differ from the reference program's by a relative error of at most 0.023.
Values may be sent and summed in bfloat16 or wider, within the bound.
No kernel may reach another device: no remote copies, remote signals or barrier semaphores. Data moves between devices by JAX's collectives and lax.ppermute only.
A program may use at most 32 MiB of HBM per device.

```python
import math
import jax
import jax.numpy as jnp
from jax import lax

D = 16384
HIST = 16
TOKENS = 1280
N_ROW = 32
N_COL = 32


def with_ends(entries, own_key, least, largest):
    longest = entries.shape.index(max(entries.shape))
    spots = []
    for shift in (0, 1):
        where = [jax.random.randint(jax.random.fold_in(own_key, axis), (), 0, length) for axis, length in enumerate(entries.shape)]
        where[longest] = (where[longest] + shift) % entries.shape[longest]
        spots.append(tuple(where))
    return entries.at[spots[0]].set(least).at[spots[1]].set(largest)


def shard_levels(own_key, dims, shards, smallest, largest):
    loudness = 1.0
    for axis_at, shards_of in shards:
        steps = jax.random.uniform(jax.random.fold_in(jax.random.fold_in(own_key, 6), axis_at), (shards_of,), jnp.float32, smallest / len(shards), largest / len(shards))
        loudness = loudness * jnp.repeat(jnp.exp(steps), dims[axis_at] // shards_of).reshape((-1,) + (1,) * (len(dims) - 1 - axis_at))
    return loudness


def scatter_about(key, dims, width, bound, pieces=(), kind=jnp.bfloat16):
    entries = width * jax.random.normal(key, dims, jnp.float32)
    if pieces:
        entries = entries * shard_levels(key, dims, pieces, -0.22, 0.18)
    return jnp.clip(entries, -bound, bound).astype(kind)


def setup_inputs(seed: int = 0) -> dict:
    streams_of = jax.random.split(jax.random.key(seed), 9)
    return {
        "saved_input": scatter_about(streams_of[0], (TOKENS, D), 1.0, 6.0, ((0, 32), (1, 32)), jnp.float32),
        "out_grad": scatter_about(streams_of[1], (TOKENS, D), 0.2, 1.2, ((0, 32), (1, 32)), jnp.float32),
        "weight": scatter_about(streams_of[2], (D, D), D ** -0.5, 0.046875, ((0, 32), (1, 32))),
        "history_in": jnp.clip(jnp.exp(math.log(8.0) - 1.3862944 * jax.random.uniform(streams_of[3], (N_ROW, N_COL, HIST), jnp.float32) ** shard_levels(streams_of[3], (N_ROW, N_COL, HIST), ((0, 32), (1, 32)), -0.2, 0.2)), 2.0, 8.0),
        "history_grad": jnp.clip(jnp.exp(math.log(1.6) - 1.3862944 * jax.random.uniform(streams_of[4], (N_ROW, N_COL, HIST), jnp.float32) ** shard_levels(streams_of[4], (N_ROW, N_COL, HIST), ((0, 32), (1, 32)), -0.2, 0.2)), 0.4, 1.6),
        "slot_in": with_ends(jax.random.randint(streams_of[5], (N_ROW, N_COL), 0, HIST), jax.random.fold_in(streams_of[5], 1), 0, HIST - 1).astype(jnp.int32),
        "slot_grad": with_ends(jax.random.randint(streams_of[6], (N_ROW, N_COL), 0, HIST), jax.random.fold_in(streams_of[6], 1), 0, HIST - 1).astype(jnp.int32),
        "step_count": jax.random.randint(streams_of[7], (1,), 1, HIST + 1).astype(jnp.int32),
    }


code_max = 448.0


def delayed_scale(history, slot, count):
    depth = history.shape[-1]
    entry = jnp.arange(depth).astype(jnp.int32)
    age = jnp.mod(slot[..., None] - 1 - entry, depth)
    valid = age < count[0]
    held = jnp.max(jnp.where(valid, history, jnp.float32(0.0)), axis=-1)
    return code_max / held


def updated(history, slot, amax):
    depth = history.shape[-1]
    entry = jnp.arange(depth).astype(jnp.int32)
    return jnp.where(entry == slot[..., None], amax[..., None], history)


def restore_blocks(values, scale):
    blocks_a, blocks_b = scale.shape
    shaped = values.reshape(blocks_a, values.shape[0] // blocks_a, blocks_b, values.shape[1] // blocks_b)
    factor = scale[:, None, :, None]
    codes = jnp.clip(shaped * factor, -code_max, code_max).astype(jnp.bfloat16)
    restored = codes.astype(jnp.float32) / factor
    amax = jnp.max(jnp.abs(shaped), axis=(1, 3))
    return restored.reshape(values.shape), amax


def reference(saved_input, out_grad, weight, history_in, history_grad, slot_in, slot_grad, step_count):
    scale_in = delayed_scale(history_in, slot_in, step_count)
    scale_grad = delayed_scale(history_grad, slot_grad, step_count)
    restored_in, amax_in = restore_blocks(saved_input, scale_in)
    restored_grad, amax_grad = restore_blocks(out_grad, scale_grad.T)
    weight_grad = jnp.dot(restored_grad.T, restored_in, precision=lax.Precision.HIGHEST)
    input_grad = jnp.dot(restored_grad, weight.astype(jnp.float32), precision=lax.Precision.HIGHEST).astype(jnp.bfloat16)
    new_history_in = updated(history_in, slot_in, amax_in)
    new_history_grad = updated(history_grad, slot_grad, amax_grad.T)
    return weight_grad, input_grad, new_history_in, new_history_grad
```

```python
import jax
import jax.numpy as jnp
from jax import lax
from jax.sharding import PartitionSpec as P

code_max = 448.0
bf16 = jnp.bfloat16
f32 = jnp.float32


def row_of(x, h, c):
    return ((x % 4) * 4 + h % 4) * 2 + c % 2


def col_of(y, l):
    return (y % 4) * 8 + l


def row_pairs(dx, dh, dc):
    return [
        (row_of(x, h, c), row_of(x + dx, h + dh, c + dc)) for x in range(4) for h in range(4) for c in range(2)
    ]


along_x = [[row_of(x, h, c) for x in range(4)] for h in range(4) for c in range(2)]
along_y = [[col_of(y, l) for y in range(4)] for l in range(8)]
quads = [[col_of(y, 4 * s + k) for k in range(4)] for y in range(4) for s in range(2)]
halves = [(col_of(y, l), col_of(y, l ^ 4)) for y in range(4) for l in range(8)]


def delayed_scale(history, slot, count):
    depth = history.shape[-1]
    entry = jnp.arange(depth)
    age = jnp.mod(slot[..., None] - 1 - entry, depth)
    valid = age < count[0]
    held = jnp.max(jnp.where(valid, history, jnp.float32(0.0)), axis=-1)
    return code_max / held


def updated(history, slot, amax):
    depth = history.shape[-1]
    entry = jnp.arange(depth)
    return jnp.where(entry == slot[..., None], amax.reshape(1, 1, 1), history)


def restore(values, history, slot, count):
    scale = delayed_scale(history, slot, count).reshape(1)[0]
    codes = jnp.clip(values * scale, -code_max, code_max).astype(bf16)
    amax = jnp.max(jnp.abs(values))
    return (codes.astype(f32) / scale).astype(bf16), updated(history, slot, amax)


def spread(block, axis_name, groups):
    n = len(groups[0])
    copies = jnp.broadcast_to(block[None], (n, *block.shape))
    return lax.all_to_all(copies, axis_name, 0, 0, axis_index_groups=groups)


def shards(saved_input, out_grad, weight, history_in, history_grad, slot_in, slot_grad, step_count):
    row = lax.axis_index("row")
    col = lax.axis_index("col")
    h = row // 2 % 4
    core = row % 2
    side = col % 8 // 4

    grad, new_history_grad = restore(out_grad, history_grad, slot_grad, step_count)
    kept, new_history_in = restore(saved_input, history_in, slot_in, step_count)

    with jax.named_scope("grad_z"):
        far = lax.ppermute(grad, "col", halves)
        first = side == 0
        pair = jnp.stack([jnp.where(first, grad, far), jnp.where(first, far, grad)])
        line = spread(pair.reshape(80, 512), "col", quads)
    with jax.named_scope("in_z"):
        moved = [lax.ppermute(kept, "row", row_pairs(0, d, 0)) for d in (2, 1, 3)]
    with jax.named_scope("grad_y"):
        grads = spread(line.reshape(320, 512), "col", along_y)
    grads = grads.reshape(4, 2, 2, 80, 512)
    own = lax.dynamic_index_in_dim(grads, core, 2, keepdims=False).reshape(640, 512)
    other = lax.dynamic_index_in_dim(grads, 1 - core, 2, keepdims=False).reshape(640, 512)

    with jax.named_scope("sum_core"):
        sent = jnp.dot(other, weight, preferred_element_type=f32).astype(bf16)
        got = lax.ppermute(sent, "row", row_pairs(0, 0, 1))
        part = jnp.dot(own, weight, preferred_element_type=f32) + got.astype(f32)
    with jax.named_scope("sum_x"):
        across = lax.all_to_all(
            part.astype(bf16).reshape(4, 160, 512), "row", 0, 0, axis_index_groups=along_x
        )
        part = jnp.sum(across.astype(f32), axis=0).reshape(2, 2, 40, 512)
    with jax.named_scope("sum_z"):

        def block_of(at):
            at = at % 4
            return lax.dynamic_index_in_dim(
                lax.dynamic_index_in_dim(part, at % 2, 0, keepdims=False), at // 2, 0, keepdims=False
            )

        total = block_of(h)
        for d in (2, 1, 3):
            total += lax.ppermute(block_of(h + d).astype(bf16), "row", row_pairs(0, d, 0)).astype(f32)
        input_grad = total.astype(bf16)

    with jax.named_scope("in_x"):
        by_distance = dict(zip((2, 1, 3), moved)) | {0: kept}
        stacked = jnp.stack([by_distance[d] for d in range(4)])
        order = [lax.dynamic_index_in_dim(stacked, (h - p) % 4, 0, keepdims=False) for p in (0, 2, 1, 3)]
        lines = jnp.concatenate(order, axis=0)
        own_in = lax.all_gather(lines, "row", axis=0, tiled=True, axis_index_groups=along_x)
    with jax.named_scope("in_core"):
        other_in = lax.ppermute(own_in, "row", row_pairs(0, 0, 1))
    with jax.named_scope("outer"):
        contract = (((0,), (0,)), ((), ()))
        weight_grad = lax.dot_general(own, own_in, contract, preferred_element_type=f32)
        weight_grad += lax.dot_general(other, other_in, contract, preferred_element_type=f32)
    return (weight_grad, input_grad, new_history_in, new_history_grad)


def solution(mesh):
    return jax.shard_map(
        shards,
        mesh=mesh,
        in_specs=(
            P("row", "col"),
            P("col", "row"),
            P("row", "col"),
            P("row", "col", None),
            P("row", "col", None),
            P("row", "col"),
            P("row", "col"),
            P(),
        ),
        out_specs=(P("row", "col"), P("row", "col"), P("row", "col", None), P("row", "col", None)),
        check_vma=False,
    )
```

```python
import jax
import jax.numpy as jnp
from jax import lax
from jax.experimental import pallas as pl
from jax.experimental.pallas import tpu as pltpu
from jax.sharding import PartitionSpec as P

code_max = 448.0
bf16 = jnp.bfloat16
f32 = jnp.float32


def row_of(x, h, c):
    return ((x % 4) * 4 + h % 4) * 2 + c % 2


def col_of(y, l):
    return (y % 4) * 8 + l


def row_pairs(dx, dh, dc):
    return [
        (row_of(x, h, c), row_of(x + dx, h + dh, c + dc)) for x in range(4) for h in range(4) for c in range(2)
    ]


def col_pairs(dy):
    return [(col_of(y, l), col_of(y + dy, l)) for y in range(4) for l in range(8)]


along_x = [[row_of(x, h, c) for x in range(4)] for h in range(4) for c in range(2)]
along_z = [[row_of(x, h, c) for h in range(4)] for x in range(4) for c in range(2)]
quads = [[col_of(y, 4 * s + k) for k in range(4)] for y in range(4) for s in range(2)]
halves = [(col_of(y, l), col_of(y, l ^ 4)) for y in range(4) for l in range(8)]


def restore_kernel(count_ref, slot_ref, values_ref, history_ref, restored_ref, updated_ref):
    slot = slot_ref[0, 0]
    history = history_ref[0]
    entry = lax.broadcasted_iota(jnp.int32, history.shape, 1)
    age = jnp.bitwise_and(slot - 1 - entry, history.shape[1] - 1)
    valid = age < count_ref[0]
    held = jnp.max(jnp.where(valid, history, 0.0), axis=1, keepdims=True)
    scale = code_max / held
    values = values_ref[...]
    codes = jnp.clip(values * scale, -code_max, code_max).astype(bf16)
    restored_ref[...] = (codes.astype(f32) / scale).astype(bf16)
    amax = jnp.max(jnp.max(jnp.abs(values), axis=0, keepdims=True), axis=1, keepdims=True)
    updated_ref[0] = jnp.where(entry == slot, amax, history)


def restore(values, history, slot, count):
    smem = pl.BlockSpec(memory_space=pltpu.SMEM)
    vmem = pl.BlockSpec(memory_space=pltpu.VMEM)
    return pl.pallas_call(
        restore_kernel,
        out_shape=(
            jax.ShapeDtypeStruct(values.shape, bf16),
            jax.ShapeDtypeStruct(history.shape, f32),
        ),
        in_specs=[smem, smem, vmem, vmem],
        out_specs=(vmem, vmem),
        compiler_params=pltpu.CompilerParams(vmem_limit_bytes=4 * 2**20),
        cost_estimate=pl.CostEstimate(flops=200000, bytes_accessed=130000, transcendentals=0),
    )(count, slot, values, history)


def call(kernel, outs, smem, vmem, scratch=()):
    place = [pl.BlockSpec(memory_space=pltpu.SMEM)] * len(smem) + [pl.BlockSpec(memory_space=pltpu.VMEM)] * len(vmem)
    return pl.pallas_call(
        kernel,
        out_shape=[jax.ShapeDtypeStruct(shape, kind) for shape, kind in outs],
        in_specs=place,
        out_specs=[pl.BlockSpec(memory_space=pltpu.VMEM)] * len(outs),
        scratch_shapes=scratch,
        compiler_params=pltpu.CompilerParams(vmem_limit_bytes=16 * 2**20),
        cost_estimate=pl.CostEstimate(flops=1024, bytes_accessed=1024, transcendentals=0),
    )(*smem, *vmem)


def other_kernel(y, core, d0, d1, d2, d3, weight, own, other, sent):
    for d, ref in enumerate((d0, d1, d2, d3)):
        at = jnp.bitwise_and(y[0] - d, 3)
        for k in range(2):
            own[at, k] = ref[k, core[0]]
            other[at, k] = ref[k, 1 - core[0]]
    rows = other[...].reshape(640, 512)
    sent[...] = jnp.dot(rows, weight[...], preferred_element_type=f32).astype(bf16)


def own_kernel(x, own, weight, got, e0, e1, e2, e3, held):
    total = jnp.dot(own[...], weight[...], preferred_element_type=f32) + got[...].astype(f32)
    held[...] = total.astype(bf16).reshape(4, 160, 512)
    for e, ref in enumerate((e0, e1, e2, e3)):
        ref[...] = held[jnp.bitwise_and(x[0] + e, 3)]


def line_kernel(e0, e1, e2, e3, blocks):
    total = e0[...].astype(f32)
    for ref in (e1, e2, e3):
        total += ref[...].astype(f32)
    for k in range(2):
        for s in range(2):
            at = 40 * (2 * k + s)
            blocks[2 * s + k] = total[at : at + 40].astype(bf16)


def outer_kernel(own, own_in, other, other_in, grad):
    contract = (((0,), (0,)), ((), ()))
    grad[...] = lax.dot_general(
        own[...], own_in[...], contract, preferred_element_type=f32
    ) + lax.dot_general(other[...], other_in[...], contract, preferred_element_type=f32)


def spread(block, axis_name, groups):
    n = len(groups[0])
    copies = jnp.broadcast_to(block[None], (n, *block.shape))
    return lax.all_to_all(copies, axis_name, 0, 0, axis_index_groups=groups)


def shards(saved_input, out_grad, weight, history_in, history_grad, slot_in, slot_grad, step_count):
    row = lax.axis_index("row")
    col = lax.axis_index("col")
    h = jnp.bitwise_and(row >> 1, 3)
    core = jnp.bitwise_and(row, 1)
    first = jnp.bitwise_and(col, 4) == 0

    grad, new_history_grad = restore(out_grad, history_grad, slot_grad, step_count)
    kept, new_history_in = restore(saved_input, history_in, slot_in, step_count)

    with jax.named_scope("grad_z"):
        far = lax.ppermute(grad, "col", halves)
        pair = jnp.stack([jnp.where(first, grad, far), jnp.where(first, far, grad)])
        line = spread(pair.reshape(80, 512), "col", quads)
    line, kept = lax.optimization_barrier((line, kept))
    with jax.named_scope("grad_y"):
        line = line.reshape(320, 512)
        passed = [lax.ppermute(line, "col", col_pairs(d)) for d in (1, 2, 3)]
    with jax.named_scope("in_z"):
        lines = spread(kept, "row", along_z)
        lines = lines.reshape(2, 2, 40, 512).swapaxes(0, 1).reshape(160, 512)
    half = ((4, 2, 80, 512), bf16)
    whole = ((640, 512), bf16)
    taken = [b.reshape(2, 2, 80, 512) for b in (line, *passed)]
    own, other, sent = call(
        other_kernel, [half, half, whole], [(col >> 3).reshape(1), core.reshape(1)], [*taken, weight]
    )
    own, other = own.reshape(640, 512), other.reshape(640, 512)

    with jax.named_scope("sum_core"):
        got = lax.ppermute(sent, "row", row_pairs(0, 0, 1))
    with jax.named_scope("sum_x"):
        parts = call(
            own_kernel,
            [((160, 512), bf16)] * 4,
            [(row >> 3).reshape(1)],
            [own, weight, got],
            [pltpu.VMEM((4, 160, 512), bf16)],
        )
        across = [lax.ppermute(parts[e], "row", row_pairs(e, 0, 0)) for e in (1, 2, 3)]
        (blocks,) = call(line_kernel, [((4, 40, 512), bf16)], [], [parts[0], *across])
    blocks, lines = lax.optimization_barrier((blocks, lines))
    with jax.named_scope("sum_z"):
        across = lax.all_to_all(blocks, "row", 0, 0, axis_index_groups=along_z)
        input_grad = jnp.sum(across.astype(f32), axis=0).astype(bf16)

    with jax.named_scope("in_x"):
        own_in = lax.all_gather(lines, "row", axis=0, tiled=True, axis_index_groups=along_x)
    with jax.named_scope("in_core"):
        other_in = lax.ppermute(own_in, "row", row_pairs(0, 0, 1))
    with jax.named_scope("outer"):
        (weight_grad,) = call(outer_kernel, [((512, 512), f32)], [], [own, own_in, other, other_in])
    return (weight_grad, input_grad, new_history_in, new_history_grad)


def solution(mesh):
    return jax.shard_map(
        shards,
        mesh=mesh,
        in_specs=(
            P("row", "col"),
            P("col", "row"),
            P("row", "col"),
            P("row", "col", None),
            P("row", "col", None),
            P("row", "col"),
            P("row", "col"),
            P(),
        ),
        out_specs=(P("row", "col"), P("row", "col"), P("row", "col", None), P("row", "col", None)),
        check_vma=False,
    )
```

```python
import jax
import jax.numpy as jnp
from jax import lax
from jax.experimental import pallas as pl
from jax.experimental.pallas import tpu as pltpu
from jax.sharding import PartitionSpec as P

code_max = 448.0
bf16 = jnp.bfloat16
f32 = jnp.float32


def row_of(x, h, c):
    return ((x % 4) * 4 + h % 4) * 2 + c % 2


def col_of(y, l):
    return (y % 4) * 8 + l


def row_pairs(dc):
    return [(row_of(x, h, c), row_of(x, h, c + dc)) for x in range(4) for h in range(4) for c in range(2)]


def ring(step):
    return [
        (row_of(x, h, c), row_of(x, h + (step, -step)[c], c)) for x in range(4) for h in range(4) for c in range(2)
    ]


along_x = [[row_of(x, h, c) for x in range(4)] for h in range(4) for c in range(2)]
along_y = [[col_of(y, l) for y in range(4)] for l in range(8)]
quads = [[col_of(y, 4 * s + k) for k in range(4)] for y in range(4) for s in range(2)]
halves = [(col_of(y, l), col_of(y, l ^ 4)) for y in range(4) for l in range(8)]


def restore_kernel(count_ref, slot_ref, values_ref, history_ref, restored_ref, updated_ref):
    slot = slot_ref[0, 0]
    history = history_ref[0]
    entry = lax.broadcasted_iota(jnp.int32, history.shape, 1)
    age = jnp.bitwise_and(slot - 1 - entry, history.shape[1] - 1)
    valid = age < count_ref[0]
    held = jnp.max(jnp.where(valid, history, 0.0), axis=1, keepdims=True)
    scale = code_max / held
    values = values_ref[...]
    codes = jnp.clip(values * scale, -code_max, code_max).astype(bf16)
    restored_ref[...] = (codes.astype(f32) / scale).astype(bf16)
    amax = jnp.max(jnp.max(jnp.abs(values), axis=0, keepdims=True), axis=1, keepdims=True)
    updated_ref[0] = jnp.where(entry == slot, amax, history)


def restore(values, history, slot, count):
    smem = pl.BlockSpec(memory_space=pltpu.SMEM)
    vmem = pl.BlockSpec(memory_space=pltpu.VMEM)
    return pl.pallas_call(
        restore_kernel,
        out_shape=(
            jax.ShapeDtypeStruct(values.shape, bf16),
            jax.ShapeDtypeStruct(history.shape, f32),
        ),
        in_specs=[smem, smem, vmem, vmem],
        out_specs=(vmem, vmem),
        compiler_params=pltpu.CompilerParams(vmem_limit_bytes=4 * 2**20),
        cost_estimate=pl.CostEstimate(flops=200000, bytes_accessed=130000, transcendentals=0),
    )(count, slot, values, history)


def call(kernel, outs, smem, vmem, scratch=()):
    place = [pl.BlockSpec(memory_space=pltpu.SMEM)] * len(smem) + [pl.BlockSpec(memory_space=pltpu.VMEM)] * len(vmem)
    return pl.pallas_call(
        kernel,
        out_shape=[jax.ShapeDtypeStruct(shape, kind) for shape, kind in outs],
        in_specs=place,
        out_specs=[pl.BlockSpec(memory_space=pltpu.VMEM)] * len(outs),
        scratch_shapes=scratch,
        compiler_params=pltpu.CompilerParams(vmem_limit_bytes=16 * 2**20),
        cost_estimate=pl.CostEstimate(flops=1024, bytes_accessed=1024, transcendentals=0),
    )(*smem, *vmem)


def sort_kernel(h, core, blocks, own, other):
    for c, ref in ((core[0], own), (1 - core[0], other)):
        turn = 1 - 2 * c
        for p, (up, side) in enumerate(((turn, c), (turn, 1 - c), (2, c), (0, c))):
            to = jnp.bitwise_and(h[0] + up, 3)
            k = 2 * jnp.bitwise_and(to, 1) + side
            for y in range(4):
                ref[y, p] = blocks[y, k, to >> 1]


def other_kernel(other, weight, sent):
    sent[...] = jnp.dot(other[...], weight[...], preferred_element_type=f32).astype(bf16)


def own_kernel(own, weight, got, part):
    total = jnp.dot(own[...], weight[...], preferred_element_type=f32) + got[...].astype(f32)
    part[...] = total.astype(bf16)


def line_kernel(across, far, near, mine):
    total = across[0].astype(f32)
    for x in range(1, 4):
        total += across[x].astype(f32)
    near[0] = total[:40]
    near[1] = total[40:80]
    far[...] = total[80:120].astype(bf16)
    mine[...] = total[120:]


def near_kernel(near, got, sent):
    sent[0] = (near[0] + got[...].astype(f32)).astype(bf16)
    sent[1] = near[1].astype(bf16)


def outer_kernel(own, own_in, other, other_in, grad):
    contract = (((0,), (0,)), ((), ()))
    grad[...] = lax.dot_general(
        own[...], own_in[...], contract, preferred_element_type=f32
    ) + lax.dot_general(other[...], other_in[...], contract, preferred_element_type=f32)


def spread(block, axis_name, groups):
    n = len(groups[0])
    copies = jnp.broadcast_to(block[None], (n, *block.shape))
    return lax.all_to_all(copies, axis_name, 0, 0, axis_index_groups=groups)


def shards(saved_input, out_grad, weight, history_in, history_grad, slot_in, slot_grad, step_count):
    row = lax.axis_index("row")
    col = lax.axis_index("col")
    h = jnp.bitwise_and(row >> 1, 3).reshape(1)
    core = jnp.bitwise_and(row, 1).reshape(1)
    first = jnp.bitwise_and(col, 4) == 0

    grad, new_history_grad = restore(out_grad, history_grad, slot_grad, step_count)
    kept, new_history_in = restore(saved_input, history_in, slot_in, step_count)

    with jax.named_scope("grad_z"):
        far = lax.ppermute(grad, "col", halves)
        pair = jnp.stack([jnp.where(first, grad, far), jnp.where(first, far, grad)])
        line = spread(pair.reshape(80, 512), "col", quads)
    with jax.named_scope("in_pair"):
        both = jnp.concatenate([kept, lax.ppermute(kept, "row", row_pairs(1))])
    line, both = lax.optimization_barrier((line, both))
    with jax.named_scope("grad_y"):
        grads = spread(line.reshape(320, 512), "col", along_y)
    with jax.named_scope("in_z"):
        near_in = lax.ppermute(both, "row", ring(-1))

    shared = ((4, 4, 40, 512), bf16)
    own, other = call(sort_kernel, [shared, shared], [h, core], [grads.reshape(4, 4, 2, 40, 512)])
    own, other = own.reshape(640, 512), other.reshape(640, 512)

    with jax.named_scope("sum_core"):
        (sent,) = call(other_kernel, [((640, 512), bf16)], [], [other, weight])
        sent, near_in = lax.optimization_barrier((sent, near_in))
        got = lax.ppermute(sent, "row", row_pairs(1))
        (part,) = call(own_kernel, [((640, 512), bf16)], [], [own, weight, got])
    part, near_in = lax.optimization_barrier((part, near_in))
    with jax.named_scope("in_z"):
        far_in = lax.ppermute(near_in[:40], "row", ring(-1))
    with jax.named_scope("sum_x"):
        across = lax.all_to_all(part.reshape(4, 160, 512), "row", 0, 0, axis_index_groups=along_x)
        block = (40, 512)
        far, near, mine = call(
            line_kernel, [(block, bf16), ((2, *block), f32), (block, f32)], [], [across]
        )
    far, kept = lax.optimization_barrier((far, kept))
    with jax.named_scope("in_x"):
        lines = jnp.concatenate([near_in, far_in, kept])
        own_in = spread(lines, "row", along_x).reshape(640, 512)
    with jax.named_scope("sum_z"):
        (sent,) = call(near_kernel, [((2, *block), bf16)], [], [near, lax.ppermute(far, "row", ring(1))])
        sent, own_in = lax.optimization_barrier((sent, own_in))
        near = lax.ppermute(sent, "row", ring(1))
    with jax.named_scope("in_core"):
        other_in = lax.ppermute(own_in, "row", row_pairs(1))
    with jax.named_scope("outer"):
        (weight_grad,) = call(outer_kernel, [((512, 512), f32)], [], [own, own_in, other, other_in])
    with jax.named_scope("sum_z"):
        near, weight_grad = lax.optimization_barrier((near, weight_grad))
        got = lax.ppermute(near[1], "row", row_pairs(1))
        input_grad = (mine + near[0].astype(f32) + got.astype(f32)).astype(bf16)
    return (weight_grad, input_grad, new_history_in, new_history_grad)


def solution(mesh):
    return jax.shard_map(
        shards,
        mesh=mesh,
        in_specs=(
            P("row", "col"),
            P("col", "row"),
            P("row", "col"),
            P("row", "col", None),
            P("row", "col", None),
            P("row", "col"),
            P("row", "col"),
            P(),
        ),
        out_specs=(P("row", "col"), P("row", "col"), P("row", "col", None), P("row", "col", None)),
        check_vma=False,
    )
```

```python
import jax
import jax.numpy as jnp
from jax import lax
from jax.experimental import pallas as pl
from jax.experimental.pallas import tpu as pltpu
from jax.sharding import PartitionSpec as P

code_max = 448.0
bf16 = jnp.bfloat16
f32 = jnp.float32


def row_of(x, h, c):
    return ((x % 4) * 4 + h % 4) * 2 + c % 2


def col_of(y, l):
    return (y % 4) * 8 + l


def row_pairs(dc):
    return [(row_of(x, h, c), row_of(x, h, c + dc)) for x in range(4) for h in range(4) for c in range(2)]


def ring(step):
    return [
        (row_of(x, h, c), row_of(x, h + (step, -step)[c], c)) for x in range(4) for h in range(4) for c in range(2)
    ]


along_x = [[row_of(x, h, c) for x in range(4)] for h in range(4) for c in range(2)]
along_y = [[col_of(y, l) for y in range(4)] for l in range(8)]
quads = [[col_of(y, 4 * s + k) for k in range(4)] for y in range(4) for s in range(2)]
halves = [(col_of(y, l), col_of(y, l ^ 4)) for y in range(4) for l in range(8)]


def restore_kernel(count_ref, slot_ref, values_ref, history_ref, restored_ref, updated_ref):
    slot = slot_ref[0, 0]
    history = history_ref[0]
    entry = lax.broadcasted_iota(jnp.int32, history.shape, 1)
    age = jnp.bitwise_and(slot - 1 - entry, history.shape[1] - 1)
    valid = age < count_ref[0]
    held = jnp.max(jnp.where(valid, history, 0.0), axis=1, keepdims=True)
    scale = code_max / held
    values = values_ref[...]
    codes = jnp.clip(values * scale, -code_max, code_max).astype(bf16)
    restored_ref[...] = (codes.astype(f32) / scale).astype(bf16)
    amax = jnp.max(jnp.max(jnp.abs(values), axis=0, keepdims=True), axis=1, keepdims=True)
    updated_ref[0] = jnp.where(entry == slot, amax, history)


def restore(values, history, slot, count):
    smem = pl.BlockSpec(memory_space=pltpu.SMEM)
    vmem = pl.BlockSpec(memory_space=pltpu.VMEM)
    return pl.pallas_call(
        restore_kernel,
        out_shape=(
            jax.ShapeDtypeStruct(values.shape, bf16),
            jax.ShapeDtypeStruct(history.shape, f32),
        ),
        in_specs=[smem, smem, vmem, vmem],
        out_specs=(vmem, vmem),
        compiler_params=pltpu.CompilerParams(vmem_limit_bytes=4 * 2**20),
        cost_estimate=pl.CostEstimate(flops=200000, bytes_accessed=130000, transcendentals=0),
    )(count, slot, values, history)


def call(kernel, outs, smem, vmem, scratch=()):
    place = [pl.BlockSpec(memory_space=pltpu.SMEM)] * len(smem) + [pl.BlockSpec(memory_space=pltpu.VMEM)] * len(vmem)
    return pl.pallas_call(
        kernel,
        out_shape=[jax.ShapeDtypeStruct(shape, kind) for shape, kind in outs],
        in_specs=place,
        out_specs=[pl.BlockSpec(memory_space=pltpu.VMEM)] * len(outs),
        scratch_shapes=scratch,
        compiler_params=pltpu.CompilerParams(vmem_limit_bytes=16 * 2**20),
        cost_estimate=pl.CostEstimate(flops=1024, bytes_accessed=1024, transcendentals=0),
    )(*smem, *vmem)


def sort_kernel(h, core, blocks, own, other):
    for c, ref in ((core[0], own), (1 - core[0], other)):
        turn = 1 - 2 * c
        for p, (up, side) in enumerate(((turn, c), (turn, 1 - c), (2, c), (0, c))):
            to = jnp.bitwise_and(h[0] + up, 3)
            k = 2 * jnp.bitwise_and(to, 1) + side
            for y in range(4):
                ref[y, p] = blocks[y, k, to >> 1]


def other_kernel(other, weight, sent):
    sent[...] = jnp.dot(other[...], weight[...], preferred_element_type=f32).astype(bf16)


def own_kernel(own, weight, got, part):
    total = jnp.dot(own[...], weight[...], preferred_element_type=f32) + got[...].astype(f32)
    part[...] = total.astype(bf16)


def line_kernel(across, near_in, near, mine, sent):
    total = across[0].astype(f32)
    for x in range(1, 4):
        total += across[x].astype(f32)
    near[0] = total[:40]
    near[1] = total[40:80]
    mine[...] = total[120:]
    sent[0] = total[80:120].astype(bf16)
    sent[1] = near_in[0]


def near_kernel(near, got, near_in, paired, sent, lines):
    sent[0] = (near[0] + got[0].astype(f32)).astype(bf16)
    sent[1] = near[1].astype(bf16)
    lines[0] = near_in[0]
    lines[1] = near_in[1]
    lines[2] = got[1]
    lines[3] = paired[...]


def outer_kernel(own, own_in, other, other_in, grad):
    contract = (((0,), (0,)), ((), ()))
    grad[...] = lax.dot_general(
        own[...], own_in[...], contract, preferred_element_type=f32
    ) + lax.dot_general(other[...], other_in[...], contract, preferred_element_type=f32)


def spread(block, axis_name, groups):
    n = len(groups[0])
    copies = jnp.broadcast_to(block[None], (n, *block.shape))
    return lax.all_to_all(copies, axis_name, 0, 0, axis_index_groups=groups)


def shards(saved_input, out_grad, weight, history_in, history_grad, slot_in, slot_grad, step_count):
    row = lax.axis_index("row")
    col = lax.axis_index("col")
    h = jnp.bitwise_and(row >> 1, 3).reshape(1)
    core = jnp.bitwise_and(row, 1).reshape(1)
    first = jnp.bitwise_and(col, 4) == 0

    grad, new_history_grad = restore(out_grad, history_grad, slot_grad, step_count)
    kept, new_history_in = restore(saved_input, history_in, slot_in, step_count)

    with jax.named_scope("grad_z"):
        far = lax.ppermute(grad, "col", halves)
        pair = jnp.stack([jnp.where(first, grad, far), jnp.where(first, far, grad)])
        line = spread(pair.reshape(80, 512), "col", quads)
    with jax.named_scope("in_pair"):
        paired = lax.ppermute(kept, "row", row_pairs(1))
        both = jnp.stack([paired, kept])
    line, both = lax.optimization_barrier((line, both))
    with jax.named_scope("grad_y"):
        grads = spread(line.reshape(320, 512), "col", along_y)
    with jax.named_scope("in_z"):
        near_in = lax.ppermute(both, "row", ring(1))

    shared = ((4, 4, 40, 512), bf16)
    own, other = call(sort_kernel, [shared, shared], [h, core], [grads.reshape(4, 4, 2, 40, 512)])
    own, other = own.reshape(640, 512), other.reshape(640, 512)

    with jax.named_scope("sum_core"):
        (sent,) = call(other_kernel, [((640, 512), bf16)], [], [other, weight])
        sent, near_in = lax.optimization_barrier((sent, near_in))
        got = lax.ppermute(sent, "row", row_pairs(1))
        (part,) = call(own_kernel, [((640, 512), bf16)], [], [own, weight, got])
    block = (40, 512)
    with jax.named_scope("sum_x"):
        across = lax.all_to_all(part.reshape(4, 160, 512), "row", 0, 0, axis_index_groups=along_x)
        near, mine, sent = call(
            line_kernel, [((2, *block), f32), (block, f32), ((2, *block), bf16)], [], [across, near_in]
        )
    with jax.named_scope("sum_z"):
        got = lax.ppermute(sent, "row", ring(1))
        sent, lines = call(
            near_kernel, [((2, *block), bf16), ((4, *block), bf16)], [], [near, got, near_in, paired]
        )
        near = lax.ppermute(sent, "row", ring(1))
    with jax.named_scope("in_x"):
        other_in = lax.all_gather(lines.reshape(160, 512), "row", axis=0, tiled=True, axis_index_groups=along_x)
    near, other_in = lax.optimization_barrier((near, other_in))
    with jax.named_scope("sum_z"):
        got = lax.ppermute(near[1], "row", row_pairs(1))
        input_grad = (mine + near[0].astype(f32) + got.astype(f32)).astype(bf16)
    with jax.named_scope("in_core"):
        own_in = lax.ppermute(other_in, "row", row_pairs(1))
    with jax.named_scope("outer"):
        (weight_grad,) = call(outer_kernel, [((512, 512), f32)], [], [own, own_in, other, other_in])
    return (weight_grad, input_grad, new_history_in, new_history_grad)


def solution(mesh):
    return jax.shard_map(
        shards,
        mesh=mesh,
        in_specs=(
            P("row", "col"),
            P("col", "row"),
            P("row", "col"),
            P("row", "col", None),
            P("row", "col", None),
            P("row", "col"),
            P("row", "col"),
            P(),
        ),
        out_specs=(P("row", "col"), P("row", "col"), P("row", "col", None), P("row", "col", None)),
        check_vma=False,
    )
```

```python
import jax
import jax.numpy as jnp
from jax import lax
from jax.experimental import pallas as pl
from jax.experimental.pallas import tpu as pltpu
from jax.sharding import PartitionSpec as P

code_max = 448.0
bf16 = jnp.bfloat16
f32 = jnp.float32


def row_of(x, h, c):
    return ((x % 4) * 4 + h % 4) * 2 + c % 2


def col_of(y, l):
    return (y % 4) * 8 + l


def row_pairs(dc):
    return [(row_of(x, h, c), row_of(x, h, c + dc)) for x in range(4) for h in range(4) for c in range(2)]


def ring(step):
    return [
        (row_of(x, h, c), row_of(x, h + (step, -step)[c], c)) for x in range(4) for h in range(4) for c in range(2)
    ]


along_x = [[row_of(x, h, c) for x in range(4)] for h in range(4) for c in range(2)]
along_y = [[col_of(y, l) for y in range(4)] for l in range(8)]
quads = [[col_of(y, 4 * s + k) for k in range(4)] for y in range(4) for s in range(2)]
halves = [(col_of(y, l), col_of(y, l ^ 4)) for y in range(4) for l in range(8)]


def restore_kernel(count_ref, slot_ref, values_ref, history_ref, restored_ref, updated_ref):
    slot = slot_ref[0, 0]
    history = history_ref[0]
    entry = lax.broadcasted_iota(jnp.int32, history.shape, 1)
    age = jnp.bitwise_and(slot - 1 - entry, history.shape[1] - 1)
    valid = age < count_ref[0]
    held = jnp.max(jnp.where(valid, history, 0.0), axis=1, keepdims=True)
    scale = code_max / held
    values = values_ref[...]
    codes = jnp.clip(values * scale, -code_max, code_max).astype(bf16)
    restored_ref[...] = (codes.astype(f32) / scale).astype(bf16)
    amax = jnp.max(jnp.max(jnp.abs(values), axis=0, keepdims=True), axis=1, keepdims=True)
    updated_ref[0] = jnp.where(entry == slot, amax, history)


def restore(values, history, slot, count):
    smem = pl.BlockSpec(memory_space=pltpu.SMEM)
    vmem = pl.BlockSpec(memory_space=pltpu.VMEM)
    return pl.pallas_call(
        restore_kernel,
        out_shape=(
            jax.ShapeDtypeStruct(values.shape, bf16),
            jax.ShapeDtypeStruct(history.shape, f32),
        ),
        in_specs=[smem, smem, vmem, vmem],
        out_specs=(vmem, vmem),
        compiler_params=pltpu.CompilerParams(vmem_limit_bytes=4 * 2**20),
        cost_estimate=pl.CostEstimate(flops=200000, bytes_accessed=130000, transcendentals=0),
    )(count, slot, values, history)


def call(kernel, outs, smem, vmem, scratch=()):
    place = [pl.BlockSpec(memory_space=pltpu.SMEM)] * len(smem) + [pl.BlockSpec(memory_space=pltpu.VMEM)] * len(vmem)
    return pl.pallas_call(
        kernel,
        out_shape=[jax.ShapeDtypeStruct(shape, kind) for shape, kind in outs],
        in_specs=place,
        out_specs=[pl.BlockSpec(memory_space=pltpu.VMEM)] * len(outs),
        scratch_shapes=scratch,
        compiler_params=pltpu.CompilerParams(vmem_limit_bytes=16 * 2**20),
        cost_estimate=pl.CostEstimate(flops=1024, bytes_accessed=1024, transcendentals=0),
    )(*smem, *vmem)


def sort_kernel(h, core, blocks, own, other):
    for c, ref in ((core[0], own), (1 - core[0], other)):
        turn = 1 - 2 * c
        for p, (up, side) in enumerate(((turn, c), (turn, 1 - c), (0, c), (2, c))):
            to = jnp.bitwise_and(h[0] + up, 3)
            k = 2 * jnp.bitwise_and(to, 1) + side
            for y in range(4):
                ref[y, p] = blocks[y, k, to >> 1]


def other_kernel(other, weight, sent):
    sent[...] = jnp.dot(other[...], weight[...], preferred_element_type=f32).astype(bf16)


def own_kernel(own, weight, got, part):
    total = jnp.dot(own[...], weight[...], preferred_element_type=f32) + got[...].astype(f32)
    part[...] = total.astype(bf16)


def line_kernel(across, near_in, paired, near, mine, sent, lines):
    total = across[0].astype(f32)
    for x in range(1, 4):
        total += across[x].astype(f32)
    near[0] = total[:40]
    near[1] = total[40:80]
    mine[...] = total[80:120]
    sent[0] = total[120:].astype(bf16)
    sent[1] = near_in[0]
    lines[0] = near_in[0]
    lines[1] = near_in[1]
    lines[2] = paired[...]


def near_kernel(near, got, sent, far):
    sent[0] = (near[0] + got[0].astype(f32)).astype(bf16)
    sent[1] = near[1].astype(bf16)
    far[...] = got[1]


def outer_kernel(own, own_in, other, other_in, grad):
    contract = (((0,), (0,)), ((), ()))
    grad[...] = lax.dot_general(
        own[...], own_in[...], contract, preferred_element_type=f32
    ) + lax.dot_general(other[...], other_in[...], contract, preferred_element_type=f32)


def spread(block, axis_name, groups):
    n = len(groups[0])
    copies = jnp.broadcast_to(block[None], (n, *block.shape))
    return lax.all_to_all(copies, axis_name, 0, 0, axis_index_groups=groups)


def shards(saved_input, out_grad, weight, history_in, history_grad, slot_in, slot_grad, step_count):
    row = lax.axis_index("row")
    col = lax.axis_index("col")
    h = jnp.bitwise_and(row >> 1, 3).reshape(1)
    core = jnp.bitwise_and(row, 1).reshape(1)
    first = jnp.bitwise_and(col, 4) == 0

    grad, new_history_grad = restore(out_grad, history_grad, slot_grad, step_count)
    kept, new_history_in = restore(saved_input, history_in, slot_in, step_count)

    with jax.named_scope("grad_z"):
        far = lax.ppermute(grad, "col", halves)
        pair = jnp.stack([jnp.where(first, grad, far), jnp.where(first, far, grad)])
        line = spread(pair.reshape(80, 512), "col", quads)
    with jax.named_scope("in_pair"):
        paired = lax.ppermute(kept, "row", row_pairs(1))
        both = jnp.stack([paired, kept])
    line, both = lax.optimization_barrier((line, both))
    with jax.named_scope("grad_y"):
        grads = spread(line.reshape(320, 512), "col", along_y)
    with jax.named_scope("in_z"):
        near_in = lax.ppermute(both, "row", ring(1))

    shared = ((4, 4, 40, 512), bf16)
    own, other = call(sort_kernel, [shared, shared], [h, core], [grads.reshape(4, 4, 2, 40, 512)])
    own, other = own.reshape(640, 512), other.reshape(640, 512)

    with jax.named_scope("sum_core"):
        (sent,) = call(other_kernel, [((640, 512), bf16)], [], [other, weight])
        sent, near_in = lax.optimization_barrier((sent, near_in))
        got = lax.ppermute(sent, "row", row_pairs(1))
        (part,) = call(own_kernel, [((640, 512), bf16)], [], [own, weight, got])
    block = (40, 512)
    with jax.named_scope("sum_x"):
        across = lax.all_to_all(part.reshape(4, 160, 512), "row", 0, 0, axis_index_groups=along_x)
        near, mine, sent, lines = call(
            line_kernel,
            [((2, *block), f32), (block, f32), ((2, *block), bf16), ((3, *block), bf16)],
            [],
            [across, near_in, paired],
        )
    with jax.named_scope("in_x"):
        most_in = lax.all_gather(lines, "row", axis=0, axis_index_groups=along_x)
    with jax.named_scope("sum_z"):
        got = lax.ppermute(sent, "row", ring(1))
        sent, last_in = call(near_kernel, [((2, *block), bf16), (block, bf16)], [], [near, got])
        sent, most_in = lax.optimization_barrier((sent, most_in))
        near = lax.ppermute(sent, "row", ring(1))
    with jax.named_scope("in_x"):
        last_in = lax.all_gather(last_in, "row", axis=0, axis_index_groups=along_x)
        other_in = jnp.concatenate([most_in, last_in[:, None]], axis=1).reshape(640, 512)
    near, other_in = lax.optimization_barrier((near, other_in))
    with jax.named_scope("in_core"):
        own_in = lax.ppermute(other_in, "row", row_pairs(1))
    with jax.named_scope("sum_z"):
        got = lax.ppermute(near[1], "row", row_pairs(1))
        input_grad = (mine + near[0].astype(f32) + got.astype(f32)).astype(bf16)
    with jax.named_scope("outer"):
        (weight_grad,) = call(outer_kernel, [((512, 512), f32)], [], [own, own_in, other, other_in])
    return (weight_grad, input_grad, new_history_in, new_history_grad)


def solution(mesh):
    return jax.shard_map(
        shards,
        mesh=mesh,
        in_specs=(
            P("row", "col"),
            P("col", "row"),
            P("row", "col"),
            P("row", "col", None),
            P("row", "col", None),
            P("row", "col"),
            P("row", "col"),
            P(),
        ),
        out_specs=(P("row", "col"), P("row", "col"), P("row", "col", None), P("row", "col", None)),
        check_vma=False,
    )
```

```python
import jax
import jax.numpy as jnp
from jax import lax
from jax.experimental import pallas as pl
from jax.experimental.pallas import tpu as pltpu
from jax.sharding import PartitionSpec as P

code_max = 448.0
bf16 = jnp.bfloat16
f32 = jnp.float32


def row_of(x, h, c):
    return ((x % 4) * 4 + h % 4) * 2 + c % 2


def col_of(y, l):
    return (y % 4) * 8 + l


def row_pairs(dc):
    return [(row_of(x, h, c), row_of(x, h, c + dc)) for x in range(4) for h in range(4) for c in range(2)]


def ring(step):
    return [
        (row_of(x, h, c), row_of(x, h + (step, -step)[c], c)) for x in range(4) for h in range(4) for c in range(2)
    ]


along_x = [[row_of(x, h, c) for x in range(4)] for h in range(4) for c in range(2)]
along_y = [[col_of(y, l) for y in range(4)] for l in range(8)]
quads = [[col_of(y, 4 * s + k) for k in range(4)] for y in range(4) for s in range(2)]
halves = [(col_of(y, l), col_of(y, l ^ 4)) for y in range(4) for l in range(8)]


def restore_kernel(count_ref, slot_ref, values_ref, history_ref, restored_ref, updated_ref):
    slot = slot_ref[0, 0]
    history = history_ref[0]
    entry = lax.broadcasted_iota(jnp.int32, history.shape, 1)
    age = jnp.bitwise_and(slot - 1 - entry, history.shape[1] - 1)
    valid = age < count_ref[0]
    held = jnp.max(jnp.where(valid, history, 0.0), axis=1, keepdims=True)
    scale = code_max / held
    values = values_ref[...]
    codes = jnp.clip(values * scale, -code_max, code_max).astype(bf16)
    restored_ref[...] = (codes.astype(f32) / scale).astype(bf16)
    amax = jnp.max(jnp.max(jnp.abs(values), axis=0, keepdims=True), axis=1, keepdims=True)
    updated_ref[0] = jnp.where(entry == slot, amax, history)


def restore(values, history, slot, count):
    smem = pl.BlockSpec(memory_space=pltpu.SMEM)
    vmem = pl.BlockSpec(memory_space=pltpu.VMEM)
    return pl.pallas_call(
        restore_kernel,
        out_shape=(
            jax.ShapeDtypeStruct(values.shape, bf16),
            jax.ShapeDtypeStruct(history.shape, f32),
        ),
        in_specs=[smem, smem, vmem, vmem],
        out_specs=(vmem, vmem),
        compiler_params=pltpu.CompilerParams(vmem_limit_bytes=4 * 2**20),
        cost_estimate=pl.CostEstimate(flops=200000, bytes_accessed=130000, transcendentals=0),
    )(count, slot, values, history)


def call(kernel, outs, smem, vmem, scratch=()):
    place = [pl.BlockSpec(memory_space=pltpu.SMEM)] * len(smem) + [pl.BlockSpec(memory_space=pltpu.VMEM)] * len(vmem)
    return pl.pallas_call(
        kernel,
        out_shape=[jax.ShapeDtypeStruct(shape, kind) for shape, kind in outs],
        in_specs=place,
        out_specs=[pl.BlockSpec(memory_space=pltpu.VMEM)] * len(outs),
        scratch_shapes=scratch,
        compiler_params=pltpu.CompilerParams(vmem_limit_bytes=16 * 2**20),
        cost_estimate=pl.CostEstimate(flops=1024, bytes_accessed=1024, transcendentals=0),
    )(*smem, *vmem)


def sort_kernel(h, core, blocks, own, other):
    for c, ref in ((core[0], own), (1 - core[0], other)):
        turn = 1 - 2 * c
        for p, (up, side) in enumerate(((turn, c), (turn, 1 - c), (2, c), (0, c))):
            to = jnp.bitwise_and(h[0] + up, 3)
            k = 2 * jnp.bitwise_and(to, 1) + side
            for y in range(4):
                ref[y, p] = blocks[y, k, to >> 1]


def other_kernel(other, weight, sent):
    sent[...] = jnp.dot(other[...], weight[...], preferred_element_type=f32).astype(bf16)


def own_kernel(own, weight, got, part):
    total = jnp.dot(own[...], weight[...], preferred_element_type=f32) + got[...].astype(f32)
    part[...] = total.astype(bf16)


def line_kernel(across, near, mine, sent):
    total = across[0].astype(f32)
    for x in range(1, 4):
        total += across[x].astype(f32)
    near[0] = total[:40]
    near[1] = total[40:80]
    mine[...] = total[120:]
    sent[...] = total[80:120].astype(bf16)


def near_kernel(near, got, sent):
    sent[0] = (near[0] + got[...].astype(f32)).astype(bf16)
    sent[1] = near[1].astype(bf16)


def lines_kernel(near_in, far_in, paired, lines):
    lines[0] = near_in[0]
    lines[1] = near_in[1]
    lines[2] = far_in[...]
    lines[3] = paired[...]


def outer_kernel(own, own_in, other, other_in, grad):
    contract = (((0,), (0,)), ((), ()))
    grad[...] = lax.dot_general(
        own[...], own_in[...], contract, preferred_element_type=f32
    ) + lax.dot_general(other[...], other_in[...], contract, preferred_element_type=f32)


def spread(block, axis_name, groups):
    n = len(groups[0])
    copies = jnp.broadcast_to(block[None], (n, *block.shape))
    return lax.all_to_all(copies, axis_name, 0, 0, axis_index_groups=groups)


def shards(saved_input, out_grad, weight, history_in, history_grad, slot_in, slot_grad, step_count):
    row = lax.axis_index("row")
    col = lax.axis_index("col")
    h = jnp.bitwise_and(row >> 1, 3).reshape(1)
    core = jnp.bitwise_and(row, 1).reshape(1)
    first = jnp.bitwise_and(col, 4) == 0

    grad, new_history_grad = restore(out_grad, history_grad, slot_grad, step_count)
    kept, new_history_in = restore(saved_input, history_in, slot_in, step_count)

    with jax.named_scope("grad_z"):
        far = lax.ppermute(grad, "col", halves)
        pair = jnp.stack([jnp.where(first, grad, far), jnp.where(first, far, grad)])
        line = spread(pair.reshape(80, 512), "col", quads)
    with jax.named_scope("in_pair"):
        paired = lax.ppermute(kept, "row", row_pairs(1))
        both = jnp.stack([paired, kept])
    line, both = lax.optimization_barrier((line, both))
    with jax.named_scope("grad_y"):
        grads = spread(line.reshape(320, 512), "col", along_y)
    with jax.named_scope("in_z"):
        near_in = lax.ppermute(both, "row", ring(1))

    shared = ((4, 4, 40, 512), bf16)
    own, other = call(sort_kernel, [shared, shared], [h, core], [grads.reshape(4, 4, 2, 40, 512)])
    own, other = own.reshape(640, 512), other.reshape(640, 512)

    with jax.named_scope("sum_core"):
        (sent,) = call(other_kernel, [((640, 512), bf16)], [], [other, weight])
        sent, near_in = lax.optimization_barrier((sent, near_in))
        got = lax.ppermute(sent, "row", row_pairs(1))
        (part,) = call(own_kernel, [((640, 512), bf16)], [], [own, weight, got])
    block = (40, 512)
    part, near_in = lax.optimization_barrier((part, near_in))
    with jax.named_scope("in_z"):
        far_in = lax.ppermute(near_in[0], "row", ring(1))
    with jax.named_scope("sum_x"):
        across = lax.all_to_all(part.reshape(4, 160, 512), "row", 0, 0, axis_index_groups=along_x)
        near, mine, sent = call(line_kernel, [((2, *block), f32), (block, f32), (block, bf16)], [], [across])
    sent, paired = lax.optimization_barrier((sent, paired))
    with jax.named_scope("in_x"):
        (lines,) = call(lines_kernel, [((4, *block), bf16)], [], [near_in, far_in, paired])
        other_in = lax.all_gather(lines.reshape(160, 512), "row", axis=0, tiled=True, axis_index_groups=along_x)
    with jax.named_scope("sum_z"):
        got = lax.ppermute(sent, "row", ring(1))
        (sent,) = call(near_kernel, [((2, *block), bf16)], [], [near, got])
        sent, other_in = lax.optimization_barrier((sent, other_in))
        near = lax.ppermute(sent, "row", ring(1))
    with jax.named_scope("in_core"):
        own_in = lax.ppermute(other_in, "row", row_pairs(1))
    with jax.named_scope("outer"):
        (weight_grad,) = call(outer_kernel, [((512, 512), f32)], [], [own, own_in, other, other_in])
    with jax.named_scope("sum_z"):
        near, weight_grad = lax.optimization_barrier((near, weight_grad))
        got = lax.ppermute(near[1], "row", row_pairs(1))
        input_grad = (mine + near[0].astype(f32) + got.astype(f32)).astype(bf16)
    return (weight_grad, input_grad, new_history_in, new_history_grad)


def solution(mesh):
    return jax.shard_map(
        shards,
        mesh=mesh,
        in_specs=(
            P("row", "col"),
            P("col", "row"),
            P("row", "col"),
            P("row", "col", None),
            P("row", "col", None),
            P("row", "col"),
            P("row", "col"),
            P(),
        ),
        out_specs=(P("row", "col"), P("row", "col"), P("row", "col", None), P("row", "col", None)),
        check_vma=False,
    )
```

```python
import jax
import jax.numpy as jnp
from jax import lax
from jax.experimental import pallas as pl
from jax.experimental.pallas import tpu as pltpu
from jax.sharding import PartitionSpec as P

code_max = 448.0
bf16 = jnp.bfloat16
f32 = jnp.float32


def row_of(x, h, c):
    return ((x % 4) * 4 + h % 4) * 2 + c % 2


def col_of(y, l):
    return (y % 4) * 8 + l


def row_pairs(dc):
    return [(row_of(x, h, c), row_of(x, h, c + dc)) for x in range(4) for h in range(4) for c in range(2)]


def ring(step):
    return [
        (row_of(x, h, c), row_of(x, h + (step, -step)[c], c)) for x in range(4) for h in range(4) for c in range(2)
    ]


along_x = [[row_of(x, h, c) for x in range(4)] for h in range(4) for c in range(2)]
along_core = [[row_of(x, h, c) for c in range(2)] for x in range(4) for h in range(4)]
along_y = [[col_of(y, l) for y in range(4)] for l in range(8)]
quads = [[col_of(y, 4 * s + k) for k in range(4)] for y in range(4) for s in range(2)]
halves = [(col_of(y, l), col_of(y, l ^ 4)) for y in range(4) for l in range(8)]


def restore_kernel(count_ref, slot_ref, values_ref, history_ref, restored_ref, updated_ref):
    slot = slot_ref[0, 0]
    history = history_ref[0]
    entry = lax.broadcasted_iota(jnp.int32, history.shape, 1)
    age = jnp.bitwise_and(slot - 1 - entry, history.shape[1] - 1)
    valid = age < count_ref[0]
    held = jnp.max(jnp.where(valid, history, 0.0), axis=1, keepdims=True)
    scale = code_max / held
    values = values_ref[...]
    codes = jnp.clip(values * scale, -code_max, code_max).astype(bf16)
    restored_ref[...] = (codes.astype(f32) / scale).astype(bf16)
    amax = jnp.max(jnp.max(jnp.abs(values), axis=0, keepdims=True), axis=1, keepdims=True)
    updated_ref[0] = jnp.where(entry == slot, amax, history)


def restore(values, history, slot, count):
    smem = pl.BlockSpec(memory_space=pltpu.SMEM)
    vmem = pl.BlockSpec(memory_space=pltpu.VMEM)
    return pl.pallas_call(
        restore_kernel,
        out_shape=(
            jax.ShapeDtypeStruct(values.shape, bf16),
            jax.ShapeDtypeStruct(history.shape, f32),
        ),
        in_specs=[smem, smem, vmem, vmem],
        out_specs=(vmem, vmem),
        compiler_params=pltpu.CompilerParams(vmem_limit_bytes=4 * 2**20),
        cost_estimate=pl.CostEstimate(flops=200000, bytes_accessed=130000, transcendentals=0),
    )(count, slot, values, history)


def call(kernel, outs, smem, vmem, scratch=()):
    place = [pl.BlockSpec(memory_space=pltpu.SMEM)] * len(smem) + [pl.BlockSpec(memory_space=pltpu.VMEM)] * len(vmem)
    return pl.pallas_call(
        kernel,
        out_shape=[jax.ShapeDtypeStruct(shape, kind) for shape, kind in outs],
        in_specs=place,
        out_specs=[pl.BlockSpec(memory_space=pltpu.VMEM)] * len(outs),
        scratch_shapes=scratch,
        compiler_params=pltpu.CompilerParams(vmem_limit_bytes=16 * 2**20),
        cost_estimate=pl.CostEstimate(flops=1024, bytes_accessed=1024, transcendentals=0),
    )(*smem, *vmem)


def sort_kernel(h, core, blocks, own, other):
    for c, ref in ((core[0], own), (1 - core[0], other)):
        turn = 1 - 2 * c
        for p, (up, side) in enumerate(((turn, c), (turn, 1 - c), (2, c), (0, c))):
            to = jnp.bitwise_and(h[0] + up, 3)
            k = 2 * jnp.bitwise_and(to, 1) + side
            for y in range(4):
                ref[y, p] = blocks[y, k, to >> 1]


def other_kernel(other, weight, sent):
    sent[...] = jnp.dot(other[...], weight[...], preferred_element_type=f32).astype(bf16)


def own_kernel(own, weight, got, part):
    total = jnp.dot(own[...], weight[...], preferred_element_type=f32) + got[...].astype(f32)
    part[...] = total.astype(bf16)


def line_kernel(across, near, mine, sent):
    total = across[0].astype(f32)
    for x in range(1, 4):
        total += across[x].astype(f32)
    near[0] = total[:40]
    near[1] = total[40:80]
    mine[...] = total[120:]
    sent[...] = total[80:120].astype(bf16)


def near_kernel(near, got, sent):
    sent[0] = (near[0] + got[...].astype(f32)).astype(bf16)
    sent[1] = near[1].astype(bf16)


def lines_kernel(near_in, far_in, paired, lines):
    lines[0] = near_in[0]
    lines[1] = near_in[1]
    lines[2] = far_in[...]
    lines[3] = paired[...]


def outer_kernel(core, own, other, front, back, grad):
    contract = (((0,), (0,)), ((), ()))
    total = jnp.zeros(grad.shape, f32)
    for ref, at in ((own, 1 - core[0]), (other, core[0])):
        for i, part in enumerate((front, back)):
            total += lax.dot_general(
                ref[320 * i : 320 * (i + 1)], part[at], contract, preferred_element_type=f32
            )
    grad[...] = total


def spread(block, axis_name, groups):
    n = len(groups[0])
    copies = jnp.broadcast_to(block[None], (n, *block.shape))
    return lax.all_to_all(copies, axis_name, 0, 0, axis_index_groups=groups)


def shards(saved_input, out_grad, weight, history_in, history_grad, slot_in, slot_grad, step_count):
    row = lax.axis_index("row")
    col = lax.axis_index("col")
    h = jnp.bitwise_and(row >> 1, 3).reshape(1)
    core = jnp.bitwise_and(row, 1).reshape(1)
    first = jnp.bitwise_and(col, 4) == 0

    grad, new_history_grad = restore(out_grad, history_grad, slot_grad, step_count)
    kept, new_history_in = restore(saved_input, history_in, slot_in, step_count)

    with jax.named_scope("in_pair"):
        paired = lax.ppermute(kept, "row", row_pairs(1))
    with jax.named_scope("grad_z"):
        far = lax.ppermute(grad, "col", halves)
        far, paired = lax.optimization_barrier((far, paired))
        pair = jnp.stack([jnp.where(first, grad, far), jnp.where(first, far, grad)])
        line = spread(pair.reshape(80, 512), "col", quads)
    both = jnp.stack([paired, kept])
    line, both = lax.optimization_barrier((line, both))
    with jax.named_scope("grad_y"):
        grads = spread(line.reshape(320, 512), "col", along_y)
    with jax.named_scope("in_z"):
        near_in = lax.ppermute(both, "row", ring(1))

    shared = ((4, 4, 40, 512), bf16)
    own, other = call(sort_kernel, [shared, shared], [h, core], [grads.reshape(4, 4, 2, 40, 512)])
    own, other = own.reshape(640, 512), other.reshape(640, 512)

    with jax.named_scope("sum_core"):
        (sent,) = call(other_kernel, [((640, 512), bf16)], [], [other, weight])
        sent, near_in = lax.optimization_barrier((sent, near_in))
        got = lax.ppermute(sent, "row", row_pairs(1))
        (part,) = call(own_kernel, [((640, 512), bf16)], [], [own, weight, got])
    block = (40, 512)
    part, near_in = lax.optimization_barrier((part, near_in))
    with jax.named_scope("in_z"):
        far_in = lax.ppermute(near_in[0], "row", ring(1))
    with jax.named_scope("sum_x"):
        across = lax.all_to_all(part.reshape(4, 160, 512), "row", 0, 0, axis_index_groups=along_x)
        near, mine, sent = call(line_kernel, [((2, *block), f32), (block, f32), (block, bf16)], [], [across])
    sent, paired = lax.optimization_barrier((sent, paired))
    with jax.named_scope("in_x"):
        (lines,) = call(lines_kernel, [((4, *block), bf16)], [], [near_in, far_in, paired])
        other_in = lax.all_gather(lines.reshape(160, 512), "row", axis=0, tiled=True, axis_index_groups=along_x)
    with jax.named_scope("sum_z"):
        got = lax.ppermute(sent, "row", ring(1))
        (sent,) = call(near_kernel, [((2, *block), bf16)], [], [near, got])
        sent, other_in = lax.optimization_barrier((sent, other_in))
        near = lax.ppermute(sent, "row", ring(1))
    with jax.named_scope("in_core"):
        front, back = (
            lax.all_gather(half, "row", axis=0, axis_index_groups=along_core)
            for half in (other_in[:320], other_in[320:])
        )
    with jax.named_scope("outer"):
        (weight_grad,) = call(outer_kernel, [((512, 512), f32)], [core], [own, other, front, back])
    with jax.named_scope("sum_z"):
        near, weight_grad = lax.optimization_barrier((near, weight_grad))
        got = lax.all_gather(near[1], "row", axis=0, axis_index_groups=along_core)
        got = jnp.where(core[0] == 0, got[1], got[0])
        input_grad = (mine + near[0].astype(f32) + got.astype(f32)).astype(bf16)
    return (weight_grad, input_grad, new_history_in, new_history_grad)


def solution(mesh):
    return jax.shard_map(
        shards,
        mesh=mesh,
        in_specs=(
            P("row", "col"),
            P("col", "row"),
            P("row", "col"),
            P("row", "col", None),
            P("row", "col", None),
            P("row", "col"),
            P("row", "col"),
            P(),
        ),
        out_specs=(P("row", "col"), P("row", "col"), P("row", "col", None), P("row", "col", None)),
        check_vma=False,
    )
```

```python
import jax
import jax.numpy as jnp
from jax import lax
from jax.experimental import pallas as pl
from jax.experimental.pallas import tpu as pltpu
from jax.sharding import PartitionSpec as P

code_max = 448.0
bf16 = jnp.bfloat16
f32 = jnp.float32


def row_of(x, h, c):
    return ((x % 4) * 4 + h % 4) * 2 + c % 2


def col_of(y, l):
    return (y % 4) * 8 + l


def row_pairs(dc):
    return [(row_of(x, h, c), row_of(x, h, c + dc)) for x in range(4) for h in range(4) for c in range(2)]


def ring(step):
    return [
        (row_of(x, h, c), row_of(x, h + (step, -step)[c], c)) for x in range(4) for h in range(4) for c in range(2)
    ]


along_x = [[row_of(x, h, c) for x in range(4)] for h in range(4) for c in range(2)]
along_core = [[row_of(x, h, c) for c in range(2)] for x in range(4) for h in range(4)]
along_y = [[col_of(y, l) for y in range(4)] for l in range(8)]
quads = [[col_of(y, 4 * s + k) for k in range(4)] for y in range(4) for s in range(2)]
halves = [[col_of(y, k), col_of(y, k + 4)] for y in range(4) for k in range(4)]


def restore_kernel(count_ref, slot_ref, values_ref, history_ref, restored_ref, updated_ref):
    slot = slot_ref[0, 0]
    history = history_ref[0]
    entry = lax.broadcasted_iota(jnp.int32, history.shape, 1)
    age = jnp.bitwise_and(slot - 1 - entry, history.shape[1] - 1)
    valid = age < count_ref[0]
    held = jnp.max(jnp.where(valid, history, 0.0), axis=1, keepdims=True)
    scale = code_max / held
    values = values_ref[...]
    codes = jnp.clip(values * scale, -code_max, code_max).astype(bf16)
    restored_ref[...] = (codes.astype(f32) / scale).astype(bf16)
    amax = jnp.max(jnp.max(jnp.abs(values), axis=0, keepdims=True), axis=1, keepdims=True)
    updated_ref[0] = jnp.where(entry == slot, amax, history)


def restore(values, history, slot, count):
    smem = pl.BlockSpec(memory_space=pltpu.SMEM)
    vmem = pl.BlockSpec(memory_space=pltpu.VMEM)
    return pl.pallas_call(
        restore_kernel,
        out_shape=(
            jax.ShapeDtypeStruct(values.shape, bf16),
            jax.ShapeDtypeStruct(history.shape, f32),
        ),
        in_specs=[smem, smem, vmem, vmem],
        out_specs=(vmem, vmem),
        compiler_params=pltpu.CompilerParams(vmem_limit_bytes=4 * 2**20),
        cost_estimate=pl.CostEstimate(flops=200000, bytes_accessed=130000, transcendentals=0),
    )(count, slot, values, history)


def call(kernel, outs, smem, vmem, scratch=()):
    place = [pl.BlockSpec(memory_space=pltpu.SMEM)] * len(smem) + [pl.BlockSpec(memory_space=pltpu.VMEM)] * len(vmem)
    return pl.pallas_call(
        kernel,
        out_shape=[jax.ShapeDtypeStruct(shape, kind) for shape, kind in outs],
        in_specs=place,
        out_specs=[pl.BlockSpec(memory_space=pltpu.VMEM)] * len(outs),
        scratch_shapes=scratch,
        compiler_params=pltpu.CompilerParams(vmem_limit_bytes=16 * 2**20),
        cost_estimate=pl.CostEstimate(flops=1024, bytes_accessed=1024, transcendentals=0),
    )(*smem, *vmem)


def sort_kernel(h, core, blocks, own, other):
    for c, ref in ((core[0], own), (1 - core[0], other)):
        turn = 1 - 2 * c
        for p, (up, side) in enumerate(((turn, c), (turn, 1 - c), (2, c), (0, c))):
            to = jnp.bitwise_and(h[0] + up, 3)
            k = 2 * jnp.bitwise_and(to, 1) + side
            for y in range(4):
                ref[y, p] = blocks[y, k, to >> 1]


def other_kernel(other, weight, sent):
    sent[...] = jnp.dot(other[...], weight[...], preferred_element_type=f32).astype(bf16)


def own_kernel(own, weight, got, part):
    total = jnp.dot(own[...], weight[...], preferred_element_type=f32) + got[...].astype(f32)
    part[...] = total.astype(bf16)


def line_kernel(across, near, mine, sent):
    total = across[0].astype(f32)
    for x in range(1, 4):
        total += across[x].astype(f32)
    near[0] = total[:40]
    near[1] = total[40:80]
    mine[...] = total[120:]
    sent[...] = total[80:120].astype(bf16)


def near_kernel(near, got, sent):
    sent[0] = (near[0] + got[...].astype(f32)).astype(bf16)
    sent[1] = near[1].astype(bf16)


def lines_kernel(near_in, far_in, paired, lines):
    lines[0] = near_in[0]
    lines[1] = near_in[1]
    lines[2] = far_in[...]
    lines[3] = paired[...]


def outer_kernel(core, own, other, front, back, grad):
    contract = (((0,), (0,)), ((), ()))
    total = jnp.zeros(grad.shape, f32)
    for ref, at in ((own, 1 - core[0]), (other, core[0])):
        for i, part in enumerate((front, back)):
            total += lax.dot_general(
                ref[320 * i : 320 * (i + 1)], part[at], contract, preferred_element_type=f32
            )
    grad[...] = total


def spread(block, axis_name, groups):
    n = len(groups[0])
    copies = jnp.broadcast_to(block[None], (n, *block.shape))
    return lax.all_to_all(copies, axis_name, 0, 0, axis_index_groups=groups)


def shards(saved_input, out_grad, weight, history_in, history_grad, slot_in, slot_grad, step_count):
    row = lax.axis_index("row")
    h = jnp.bitwise_and(row >> 1, 3).reshape(1)
    core = jnp.bitwise_and(row, 1).reshape(1)

    grad, new_history_grad = restore(out_grad, history_grad, slot_grad, step_count)
    kept, new_history_in = restore(saved_input, history_in, slot_in, step_count)

    with jax.named_scope("grad_z"):
        pair = lax.all_gather(grad, "col", axis=0, axis_index_groups=halves)
        line = spread(pair.reshape(80, 512), "col", quads)
    with jax.named_scope("in_pair"):
        paired = lax.ppermute(kept, "row", row_pairs(1))
        both = jnp.stack([paired, kept])
    line, both = lax.optimization_barrier((line, both))
    with jax.named_scope("grad_y"):
        grads = spread(line.reshape(320, 512), "col", along_y)
    with jax.named_scope("in_z"):
        near_in = lax.ppermute(both, "row", ring(1))

    shared = ((4, 4, 40, 512), bf16)
    own, other = call(sort_kernel, [shared, shared], [h, core], [grads.reshape(4, 4, 2, 40, 512)])
    own, other = own.reshape(640, 512), other.reshape(640, 512)

    with jax.named_scope("sum_core"):
        (sent,) = call(other_kernel, [((640, 512), bf16)], [], [other, weight])
        sent, near_in = lax.optimization_barrier((sent, near_in))
        got = lax.ppermute(sent, "row", row_pairs(1))
        (part,) = call(own_kernel, [((640, 512), bf16)], [], [own, weight, got])
    block = (40, 512)
    part, near_in = lax.optimization_barrier((part, near_in))
    with jax.named_scope("in_z"):
        far_in = lax.ppermute(near_in[0], "row", ring(1))
    with jax.named_scope("sum_x"):
        across = lax.all_to_all(part.reshape(4, 160, 512), "row", 0, 0, axis_index_groups=along_x)
        near, mine, sent = call(line_kernel, [((2, *block), f32), (block, f32), (block, bf16)], [], [across])
    sent, paired = lax.optimization_barrier((sent, paired))
    with jax.named_scope("in_x"):
        (lines,) = call(lines_kernel, [((4, *block), bf16)], [], [near_in, far_in, paired])
        other_in = lax.all_gather(lines.reshape(160, 512), "row", axis=0, tiled=True, axis_index_groups=along_x)
    with jax.named_scope("sum_z"):
        got = lax.ppermute(sent, "row", ring(1))
        (sent,) = call(near_kernel, [((2, *block), bf16)], [], [near, got])
        sent, other_in = lax.optimization_barrier((sent, other_in))
        near = lax.ppermute(sent, "row", ring(1))
    with jax.named_scope("in_core"):
        front, back = (
            lax.all_gather(half, "row", axis=0, axis_index_groups=along_core)
            for half in (other_in[:320], other_in[320:])
        )
    with jax.named_scope("outer"):
        (weight_grad,) = call(outer_kernel, [((512, 512), f32)], [core], [own, other, front, back])
    with jax.named_scope("sum_z"):
        near, weight_grad = lax.optimization_barrier((near, weight_grad))
        got = lax.all_gather(near[1], "row", axis=0, axis_index_groups=along_core)
        got = jnp.where(core[0] == 0, got[1], got[0])
        input_grad = (mine + near[0].astype(f32) + got.astype(f32)).astype(bf16)
    return (weight_grad, input_grad, new_history_in, new_history_grad)


def solution(mesh):
    return jax.shard_map(
        shards,
        mesh=mesh,
        in_specs=(
            P("row", "col"),
            P("col", "row"),
            P("row", "col"),
            P("row", "col", None),
            P("row", "col", None),
            P("row", "col"),
            P("row", "col"),
            P(),
        ),
        out_specs=(P("row", "col"), P("row", "col"), P("row", "col", None), P("row", "col", None)),
        check_vma=False,
    )
```
